32 devices in a mesh: row: 8 (over z, core), col: 4 (over y, x).
Axes of the slice: x: 2, y: 2, z: 4, core: 2. Of those that a mesh axis runs over, the one named last changes fastest.
Arguments:
- inputs: bfloat16 [64, 8192], P('col', 'row'), may hold values from -6 to 6
- w_up: bfloat16 [8192, 26624], P('row', 'col'), may hold values from -0.0625 to 0.0625
- w_down: bfloat16 [26624, 8192], P('col', 'row'), may hold values from -0.0390625 to 0.0390625
- out_grad: bfloat16 [64, 8192], P('col', 'row'), may hold values from -6 to 6
Outputs:
- result: bfloat16 [64, 8192], P('col', 'row')
- in_grad: bfloat16 [64, 8192], P('col', 'row')
- up_grad: bfloat16 [8192, 26624], P('row', 'col')
- down_grad: bfloat16 [26624, 8192], P('col', 'row')
The draws below stay inside these ranges and needn't reach their ends.
All inputs are finite; a program needn't handle non-finite values.
Results may differ from the reference program's by a relative error of at most 0.005.
Values may be sent and summed in bfloat16 or wider, within the bound.
A program may use at most 128 MiB of HBM per device.

```python
import jax
import jax.numpy as jnp

D = 8192
FF = 26624
TOKENS = 64


def steps_of(own_key, dims, shards, low, high):
    loudness, own = 1.0, jax.random.fold_in(own_key, 6)
    for dim, parts in shards:
        draws = jnp.exp(jax.random.uniform(jax.random.fold_in(own, dim), (parts,), jnp.float32, low / len(shards), high / len(shards)))
        loudness = loudness * jnp.repeat(draws, dims[dim] // parts).reshape([-1 if axis == dim else 1 for axis in range(len(dims))])
    return loudness


def normal_values(rng, extent, spread, bound, split=(), kind=jnp.bfloat16):
    loudness = steps_of(rng, extent, split, -0.22, 0.18) if split else 1.0
    values = jax.random.normal(rng, extent, jnp.float32) * spread * loudness
    return jnp.minimum(jnp.maximum(values, -bound), bound).astype(kind)


def setup_inputs(seed: int = 0) -> dict:
    splits = jax.random.split(jax.random.key(seed), 5)
    inputs = normal_values(splits[0], (TOKENS, D), 1.0, 6.0, ((0, 4), (1, 8)))
    w_up = normal_values(splits[1], (D, FF), D ** -0.5, 0.0625, ((0, 8), (1, 4)))
    w_down = normal_values(splits[2], (FF, D), FF ** -0.5, 0.0390625, ((0, 4), (1, 8)))
    out_grad = normal_values(splits[3], (TOKENS, D), 1.0, 6.0, ((0, 4), (1, 8)))
    return {"inputs": inputs, "w_up": w_up, "w_down": w_down, "out_grad": out_grad}


def gelu_value(hidden):
    return 0.5 * hidden * (1.0 + jax.scipy.special.erf(hidden * 0.7071067811865476))


def gelu_slope(hidden):
    return 0.5 * (1.0 + jax.scipy.special.erf(hidden * 0.7071067811865476)) + hidden * jnp.exp(-0.5 * hidden * hidden) * 0.3989422804014327


def reference(inputs, w_up, w_down, out_grad):
    hidden = jnp.dot(inputs, w_up, preferred_element_type=jnp.float32)
    activated = gelu_value(hidden).astype(jnp.bfloat16)
    result = jnp.dot(activated, w_down, preferred_element_type=jnp.float32).astype(jnp.bfloat16)
    act_grad = jnp.dot(out_grad, w_down.T, preferred_element_type=jnp.float32)
    hid_grad = (act_grad * gelu_slope(hidden)).astype(jnp.bfloat16)
    in_grad = jnp.dot(hid_grad, w_up.T, preferred_element_type=jnp.float32).astype(jnp.bfloat16)
    up_grad = jnp.dot(inputs.T, hid_grad, preferred_element_type=jnp.float32).astype(jnp.bfloat16)
    down_grad = jnp.dot(activated.T, out_grad, preferred_element_type=jnp.float32).astype(jnp.bfloat16)
    return (result, in_grad, up_grad, down_grad)
```

```python
import functools

import jax
import jax.numpy as jnp
from jax import lax
from jax.experimental import pallas as pl
from jax.experimental.pallas import tpu as pltpu
from jax.sharding import PartitionSpec as P

MESH = pl.DeviceIdType.MESH
F32 = jnp.float32
BF16 = jnp.bfloat16


def gelu_value(hidden):
    return 0.5 * hidden * (1.0 + lax.erf(hidden * 0.7071067811865476))


def gelu_slope(hidden):
    return (
        0.5 * (1.0 + lax.erf(hidden * 0.7071067811865476))
        + hidden * jnp.exp(-0.5 * hidden * hidden) * 0.3989422804014327
    )


def contract_first(left, right):
    return lax.dot_general(
        left, right, (((0,), (0,)), ((), ())), preferred_element_type=F32
    )


def contract_last(left, right):
    return lax.dot_general(
        left, right, (((1,), (1,)), ((), ())), preferred_element_type=F32
    )


def tile_of(size):
    return 256 if size % 256 == 0 else 128


def tiles(size, body):
    tile = tile_of(size)

    @pl.loop(0, size // tile)
    def _(step):
        body(pl.ds(pl.multiple_of(step * tile, tile), tile))


def exchange_kernel(
    R, C,
    x_ref, wup_ref, wdn_ref, g_ref,
    res_ref, ing_ref, act_ref, hg_ref, xo_ref, go_ref,
    wup, wdn, xg, pair_send, pair_recv, own, zsend, zrecv, hid, half, part, csend, crecv,
    w_sem, ag_s, ag_r, pr_s, pr_r, zs_s, zs_r, za_s, za_r, sb_s, sb_r, co_s, co_r,
):
    Z = R // 2
    r, c = lax.axis_index("row"), lax.axis_index("col")
    z, core = lax.div(r, 2), lax.rem(r, 2)
    other = 1 - core
    TC, K = x_ref.shape
    T = TC * C
    TG = T // Z
    F = wup_ref.shape[1]
    W = wup.shape[2]
    skip = 2 * W - F

    def zpeer(k):
        return {"row": lax.rem(z + k, Z) * 2 + core}

    def cpeer(k):
        return {"col": lax.rem(c + k, C)}

    sibling = {"row": z * 2 + other}

    def zrows(k):
        return pl.ds(pl.multiple_of(lax.rem(z + k, Z) * TG, TG), TG)

    def crows(k):
        return pl.ds(pl.multiple_of(lax.rem(c + k, C) * TC, TC), TC)

    def remote(src, dst, ssem, rsem, peer):
        return pltpu.make_async_remote_copy(
            src_ref=src, dst_ref=dst, send_sem=ssem, recv_sem=rsem,
            device_id=peer, device_id_type=MESH,
        )

    def load(op, which):
        start = pl.multiple_of(which * (F - W), 128)
        if op == 0:
            src, dst = wup_ref.at[:, pl.ds(start, W)], wup.at[which]
        else:
            src, dst = wdn_ref.at[pl.ds(start, W), :], wdn.at[which]
        return pltpu.make_async_copy(src, dst, w_sem.at[op, which])

    loads = {}
    for op in range(2):
        for name, which in (("other", other), ("own", core)):
            loads[op, name] = load(op, which)
            loads[op, name].start()

    barrier = pltpu.get_barrier_semaphore()
    peers = [sibling] + [zpeer(k) for k in range(1, Z)] + [cpeer(k) for k in range(1, C)]
    for peer in peers:
        pl.semaphore_signal(barrier, inc=1, device_id=peer, device_id_type=MESH)
    pl.semaphore_wait(barrier, len(peers))

    sends = []

    gathers = []
    for op, ref in enumerate((x_ref, g_ref)):
        for k in range(1, C):
            copy = remote(ref, xg.at[op, crows(0)], ag_s.at[op, k], ag_r.at[op, k], cpeer(k))
            copy.start()
            gathers.append((op, copy))
            sends.append(copy)
        xg[op, crows(0), :] = ref[...]

    def partial(op, which, cols):
        if op == 0:
            return jnp.dot(xg[0], wup[which, :, cols], preferred_element_type=F32)
        return contract_last(xg[1], wdn[which, cols, :])

    zsums = {}
    for op in range(2):
        for o, copy in gathers:
            if o == op:
                copy.wait_recv()
        loads[op, "other"].wait()

        def to_send(cols, op=op):
            pair_send[op, :, cols] = partial(op, other, cols).astype(BF16)

        tiles(W, to_send)
        pair = remote(pair_send.at[op], pair_recv.at[op], pr_s.at[op], pr_r.at[op], sibling)
        pair.start()
        sends.append(pair)
        loads[op, "own"].wait()

        def to_keep(cols, op=op):
            own[op, :, cols] = partial(op, core, cols)

        tiles(W, to_keep)
        pair.wait_recv()

        def add_pair(cols, op=op):
            total = own[op, :, cols] + pair_recv[op, :, cols].astype(F32)
            own[op, :, cols] = total
            zsend[op, :, cols] = total.astype(BF16)

        tiles(W, add_pair)
        for k in range(1, Z):
            copy = remote(
                zsend.at[op, zrows(k)], zrecv.at[op, k - 1],
                zs_s.at[op, k], zs_r.at[op, k], zpeer(k),
            )
            copy.start()
            zsums[op, k] = copy
            sends.append(copy)

    spread, shared = {}, {}
    for op in range(2):
        for k in range(1, Z):
            zsums[op, k].wait_recv()

        def share(cols, op=op):
            total = own[op, zrows(0), cols]
            for k in range(1, Z):
                total = total + zrecv[op, k - 1, :, cols].astype(F32)
            if op == 0:
                hid[:, cols] = total
                total = gelu_value(total)
            else:
                total = total * gelu_slope(hid[:, cols])
            half[op, core, zrows(0), cols] = total.astype(BF16)

        tiles(W, share)
        for k in range(1, Z):
            block = half.at[op, core, zrows(0)]
            copy = remote(block, block, za_s.at[op, k], za_r.at[op, k], zpeer(k))
            copy.start()
            spread[op, k] = copy
            sends.append(copy)
        block = half.at[op, core, zrows(0)]
        copy = remote(block, block, sb_s.at[op, 0], sb_r.at[op, 0], sibling)
        copy.start()
        shared[op, 0] = copy
        sends.append(copy)

    outs = {}
    for op in range(2):
        for k in range(1, Z):
            spread[op, k].wait_recv()
            block = half.at[op, core, zrows(Z - k)]
            copy = remote(block, block, sb_s.at[op, k], sb_r.at[op, k], sibling)
            copy.start()
            shared[op, k] = copy
            sends.append(copy)
        for k in range(Z):
            shared[op, k].wait_recv()

        def project(cols, op=op):
            if op == 0:
                total = jnp.dot(half[0, 0], wdn[0, :, cols], preferred_element_type=F32)
                total += jnp.dot(
                    half[0, 1, :, skip:], wdn[1, skip:, cols], preferred_element_type=F32
                )
            else:
                total = contract_last(half[1, 0], wup[0, cols, :])
                total += contract_last(half[1, 1, :, skip:], wup[1, cols, skip:])
            part[op, :, cols] = total
            csend[op, :, cols] = total.astype(BF16)

        tiles(K, project)
        for k in range(1, C):
            copy = remote(
                csend.at[op, crows(k)], crecv.at[op, k - 1],
                co_s.at[op, k], co_r.at[op, k], cpeer(k),
            )
            copy.start()
            outs[op, k] = copy
            sends.append(copy)

    for op, ref in enumerate((act_ref, hg_ref)):
        ref[:, :W] = half[op, 0]
        ref[:, W:] = half[op, 1, :, skip:]
    xo_ref[...] = xg[0]
    go_ref[...] = xg[1]

    for op, ref in enumerate((res_ref, ing_ref)):
        total = part[op, crows(0), :]
        for k in range(1, C):
            outs[op, k].wait_recv()
            total = total + crecv[op, k - 1].astype(F32)
        ref[...] = total.astype(ref.dtype)

    for copy in sends:
        copy.wait_send()


def on_device(R, C, inputs, w_up, w_down, out_grad):
    TC, K = inputs.shape
    F = w_up.shape[1]
    T, Z = TC * C, R // 2
    TG = T // Z
    W = -(-F // 256) * 128
    vmem = pl.BlockSpec(memory_space=pltpu.VMEM)
    hbm = pl.BlockSpec(memory_space=pl.ANY)
    dma = pltpu.SemaphoreType.DMA
    shape = jax.ShapeDtypeStruct
    result, in_grad, activated, hid_grad, gathered, cotangent = pl.pallas_call(
        functools.partial(exchange_kernel, R, C),
        out_shape=[
            shape((TC, K), BF16), shape((TC, K), BF16),
            shape((T, F), BF16), shape((T, F), BF16),
            shape((T, K), BF16), shape((T, K), BF16),
        ],
        in_specs=[vmem, hbm, hbm, vmem],
        out_specs=[vmem] * 6,
        scratch_shapes=[
            pltpu.VMEM((2, K, W), BF16),
            pltpu.VMEM((2, W, K), BF16),
            pltpu.VMEM((2, T, K), BF16),
            pltpu.VMEM((2, T, W), BF16),
            pltpu.VMEM((2, T, W), BF16),
            pltpu.VMEM((2, T, W), F32),
            pltpu.VMEM((2, T, W), BF16),
            pltpu.VMEM((2, Z - 1, TG, W), BF16),
            pltpu.VMEM((TG, W), F32),
            pltpu.VMEM((2, 2, T, W), BF16),
            pltpu.VMEM((2, T, K), F32),
            pltpu.VMEM((2, T, K), BF16),
            pltpu.VMEM((2, C - 1, TC, K), BF16),
            dma((2, 2)),
            dma((2, C)), dma((2, C)),
            dma((2,)), dma((2,)),
            dma((2, Z)), dma((2, Z)),
            dma((2, Z)), dma((2, Z)),
            dma((2, Z)), dma((2, Z)),
            dma((2, C)), dma((2, C)),
        ],
        compiler_params=pltpu.CompilerParams(
            collective_id=0, has_side_effects=True, vmem_limit_bytes=56 * 2**20
        ),
        cost_estimate=pl.CostEstimate(
            flops=8 * T * K * F, bytes_accessed=4 * K * F, transcendentals=0
        ),
    )(inputs, w_up, w_down, out_grad)
    down_grad = contract_first(activated, cotangent).astype(BF16)
    up_grad = contract_first(gathered, hid_grad).astype(BF16)
    return (result, in_grad, up_grad, down_grad)


def solution(mesh):
    R, C = mesh.shape["row"], mesh.shape["col"]
    return jax.shard_map(
        functools.partial(on_device, R, C),
        mesh=mesh,
        in_specs=(P("col", "row"), P("row", "col"), P("col", "row"), P("col", "row")),
        out_specs=(P("col", "row"), P("col", "row"), P("row", "col"), P("col", "row")),
        check_vma=False,
    )
```

```python
import functools

import jax
import jax.numpy as jnp
from jax import lax
from jax.experimental import pallas as pl
from jax.experimental.pallas import tpu as pltpu
from jax.sharding import PartitionSpec as P

MESH = pl.DeviceIdType.MESH
F32 = jnp.float32
BF16 = jnp.bfloat16


def gelu_value(hidden):
    return 0.5 * hidden * (1.0 + lax.erf(hidden * 0.7071067811865476))


def gelu_slope(hidden):
    return (
        0.5 * (1.0 + lax.erf(hidden * 0.7071067811865476))
        + hidden * jnp.exp(-0.5 * hidden * hidden) * 0.3989422804014327
    )


def contract_first(left, right):
    return lax.dot_general(
        left, right, (((0,), (0,)), ((), ())), preferred_element_type=F32
    )


def contract_last(left, right):
    return lax.dot_general(
        left, right, (((1,), (1,)), ((), ())), preferred_element_type=F32
    )


def tile_of(size):
    return 256 if size % 256 == 0 else 128


def tiles(size, body):
    tile = tile_of(size)

    @pl.loop(0, size // tile)
    def _(step):
        body(pl.ds(pl.multiple_of(step * tile, tile), tile))


def exchange_kernel(
    R, C,
    x_ref, wup_ref, wdn_ref, g_ref,
    res_ref, ing_ref, act_ref, hg_ref, xo_ref, go_ref,
    wup, wdn, xg, pair_send, pair_recv, own, zsend, zrecv, hid, half, part, csend, crecv,
    w_sem, ag_s, ag_r, pr_s, pr_r, zs_s, zs_r, za_s, za_r, sb_s, sb_r, co_s, co_r,
):
    Z = R // 2
    r, c = lax.axis_index("row"), lax.axis_index("col")
    z, core = lax.div(r, 2), lax.rem(r, 2)
    other = 1 - core
    TC, K = x_ref.shape
    T = TC * C
    TG = T // Z
    F = wup_ref.shape[1]
    W = wup.shape[2]
    skip = 2 * W - F

    def zpeer(k):
        return {"row": lax.rem(z + k, Z) * 2 + core}

    def cpeer(k):
        return {"col": lax.rem(c + k, C)}

    sibling = {"row": z * 2 + other}

    def zrows(k):
        return pl.ds(pl.multiple_of(lax.rem(z + k, Z) * TG, TG), TG)

    def crows(k):
        return pl.ds(pl.multiple_of(lax.rem(c + k, C) * TC, TC), TC)

    def remote(src, dst, ssem, rsem, peer):
        return pltpu.make_async_remote_copy(
            src_ref=src, dst_ref=dst, send_sem=ssem, recv_sem=rsem,
            device_id=peer, device_id_type=MESH,
        )

    def load(op, which):
        start = pl.multiple_of(which * (F - W), 128)
        if op == 0:
            src, dst = wup_ref.at[:, pl.ds(start, W)], wup.at[which]
        else:
            src, dst = wdn_ref.at[pl.ds(start, W), :], wdn.at[which]
        return pltpu.make_async_copy(src, dst, w_sem.at[op, which])

    loads = {}
    for op in range(2):
        for name, which in (("other", other), ("own", core)):
            loads[op, name] = load(op, which)
            loads[op, name].start()

    barrier = pltpu.get_barrier_semaphore()
    peers = [sibling] + [zpeer(k) for k in range(1, Z)] + [cpeer(k) for k in range(1, C)]
    for peer in peers:
        pl.semaphore_signal(barrier, inc=1, device_id=peer, device_id_type=MESH)
    pl.semaphore_wait(barrier, len(peers))

    sends = []

    gathers = []
    for op, ref in enumerate((x_ref, g_ref)):
        for k in range(1, C):
            copy = remote(ref, xg.at[op, crows(0)], ag_s.at[op, k], ag_r.at[op, k], cpeer(k))
            copy.start()
            gathers.append((op, copy))
            sends.append(copy)
        xg[op, crows(0), :] = ref[...]

    def partial(op, which, cols):
        if op == 0:
            return jnp.dot(xg[0], wup[which, :, cols], preferred_element_type=F32)
        return contract_last(xg[1], wdn[which, cols, :])

    zsums = {}
    for op in range(2):
        for o, copy in gathers:
            if o == op:
                copy.wait_recv()
        loads[op, "other"].wait()

        def to_send(cols, op=op):
            pair_send[op, :, cols] = partial(op, other, cols).astype(BF16)

        tiles(W, to_send)
        pair = remote(pair_send.at[op], pair_recv.at[op], pr_s.at[op], pr_r.at[op], sibling)
        pair.start()
        sends.append(pair)
        loads[op, "own"].wait()

        def to_keep(cols, op=op):
            own[op, :, cols] = partial(op, core, cols)

        tiles(W, to_keep)
        pair.wait_recv()

        def add_pair(cols, op=op):
            total = own[op, :, cols] + pair_recv[op, :, cols].astype(F32)
            own[op, :, cols] = total
            zsend[op, :, cols] = total.astype(BF16)

        tiles(W, add_pair)
        for k in range(1, Z):
            copy = remote(
                zsend.at[op, zrows(k)], zrecv.at[op, k - 1],
                zs_s.at[op, k], zs_r.at[op, k], zpeer(k),
            )
            copy.start()
            zsums[op, k] = copy
            sends.append(copy)

    spread, shared = {}, {}
    for op in range(2):
        for k in range(1, Z):
            zsums[op, k].wait_recv()

        def share(cols, op=op):
            total = own[op, zrows(0), cols]
            for k in range(1, Z):
                total = total + zrecv[op, k - 1, :, cols].astype(F32)
            if op == 0:
                hid[:, cols] = total
                total = gelu_value(total)
            else:
                total = total * gelu_slope(hid[:, cols])
            half[op, core, zrows(0), cols] = total.astype(BF16)

        tiles(W, share)
        for k in range(1, Z):
            block = half.at[op, core, zrows(0)]
            copy = remote(block, block, za_s.at[op, k], za_r.at[op, k], zpeer(k))
            copy.start()
            spread[op, k] = copy
            sends.append(copy)
        block = half.at[op, core, zrows(0)]
        copy = remote(block, block, sb_s.at[op, 0], sb_r.at[op, 0], sibling)
        copy.start()
        shared[op, 0] = copy
        sends.append(copy)

    outs = {}
    for op in range(2):
        for k in range(1, Z):
            spread[op, k].wait_recv()
            block = half.at[op, core, zrows(Z - k)]
            copy = remote(block, block, sb_s.at[op, k], sb_r.at[op, k], sibling)
            copy.start()
            shared[op, k] = copy
            sends.append(copy)
        for k in range(Z):
            shared[op, k].wait_recv()

        def project(cols, op=op):
            if op == 0:
                total = jnp.dot(half[0, 0], wdn[0, :, cols], preferred_element_type=F32)
                total += jnp.dot(
                    half[0, 1, :, skip:], wdn[1, skip:, cols], preferred_element_type=F32
                )
            else:
                total = contract_last(half[1, 0], wup[0, cols, :])
                total += contract_last(half[1, 1, :, skip:], wup[1, cols, skip:])
            part[op, :, cols] = total
            csend[op, :, cols] = total.astype(BF16)

        tiles(K, project)
        for k in range(1, C):
            copy = remote(
                csend.at[op, crows(k)], crecv.at[op, k - 1],
                co_s.at[op, k], co_r.at[op, k], cpeer(k),
            )
            copy.start()
            outs[op, k] = copy
            sends.append(copy)

    for op, ref in enumerate((act_ref, hg_ref)):
        ref[:, :W] = half[op, 0]
        ref[:, W:] = half[op, 1, :, skip:]
    xo_ref[...] = xg[0]
    go_ref[...] = xg[1]

    for op, ref in enumerate((res_ref, ing_ref)):
        total = part[op, crows(0), :]
        for k in range(1, C):
            outs[op, k].wait_recv()
            total = total + crecv[op, k - 1].astype(F32)
        ref[...] = total.astype(ref.dtype)

    for copy in sends:
        copy.wait_send()


def grads_kernel(x_ref, h_ref, a_ref, g_ref, up_ref, down_ref):
    up_ref[...] = contract_first(x_ref[...], h_ref[...]).astype(BF16)
    down_ref[...] = contract_first(a_ref[...], g_ref[...]).astype(BF16)


def weight_grads(gathered, hid_grad, activated, cotangent):
    T, K = gathered.shape
    F = hid_grad.shape[1]
    tile = 512 if F % 512 == 0 else 128
    whole = pl.BlockSpec((T, K), lambda i: (0, 0))
    piece = pl.BlockSpec((T, tile), lambda i: (0, i))
    return pl.pallas_call(
        grads_kernel,
        grid=(F // tile,),
        out_shape=[
            jax.ShapeDtypeStruct((K, F), BF16), jax.ShapeDtypeStruct((F, K), BF16),
        ],
        in_specs=[whole, piece, piece, whole],
        out_specs=[
            pl.BlockSpec((K, tile), lambda i: (0, i)),
            pl.BlockSpec((tile, K), lambda i: (i, 0)),
        ],
        compiler_params=pltpu.CompilerParams(vmem_limit_bytes=40 * 2**20),
        cost_estimate=pl.CostEstimate(
            flops=4 * T * K * F, bytes_accessed=4 * K * F, transcendentals=0
        ),
    )(gathered, hid_grad, activated, cotangent)


def on_device(R, C, inputs, w_up, w_down, out_grad):
    TC, K = inputs.shape
    F = w_up.shape[1]
    T, Z = TC * C, R // 2
    TG = T // Z
    W = -(-F // 256) * 128
    vmem = pl.BlockSpec(memory_space=pltpu.VMEM)
    hbm = pl.BlockSpec(memory_space=pl.ANY)
    dma = pltpu.SemaphoreType.DMA
    shape = jax.ShapeDtypeStruct
    result, in_grad, activated, hid_grad, gathered, cotangent = pl.pallas_call(
        functools.partial(exchange_kernel, R, C),
        out_shape=[
            shape((TC, K), BF16), shape((TC, K), BF16),
            shape((T, F), BF16), shape((T, F), BF16),
            shape((T, K), BF16), shape((T, K), BF16),
        ],
        in_specs=[vmem, hbm, hbm, vmem],
        out_specs=[vmem] * 6,
        scratch_shapes=[
            pltpu.VMEM((2, K, W), BF16),
            pltpu.VMEM((2, W, K), BF16),
            pltpu.VMEM((2, T, K), BF16),
            pltpu.VMEM((2, T, W), BF16),
            pltpu.VMEM((2, T, W), BF16),
            pltpu.VMEM((2, T, W), F32),
            pltpu.VMEM((2, T, W), BF16),
            pltpu.VMEM((2, Z - 1, TG, W), BF16),
            pltpu.VMEM((TG, W), F32),
            pltpu.VMEM((2, 2, T, W), BF16),
            pltpu.VMEM((2, T, K), F32),
            pltpu.VMEM((2, T, K), BF16),
            pltpu.VMEM((2, C - 1, TC, K), BF16),
            dma((2, 2)),
            dma((2, C)), dma((2, C)),
            dma((2,)), dma((2,)),
            dma((2, Z)), dma((2, Z)),
            dma((2, Z)), dma((2, Z)),
            dma((2, Z)), dma((2, Z)),
            dma((2, C)), dma((2, C)),
        ],
        compiler_params=pltpu.CompilerParams(
            collective_id=0, has_side_effects=True, vmem_limit_bytes=56 * 2**20
        ),
        cost_estimate=pl.CostEstimate(
            flops=8 * T * K * F, bytes_accessed=4 * K * F, transcendentals=0
        ),
    )(inputs, w_up, w_down, out_grad)
    up_grad, down_grad = weight_grads(gathered, hid_grad, activated, cotangent)
    return (result, in_grad, up_grad, down_grad)


def solution(mesh):
    R, C = mesh.shape["row"], mesh.shape["col"]
    return jax.shard_map(
        functools.partial(on_device, R, C),
        mesh=mesh,
        in_specs=(P("col", "row"), P("row", "col"), P("col", "row"), P("col", "row")),
        out_specs=(P("col", "row"), P("col", "row"), P("row", "col"), P("col", "row")),
        check_vma=False,
    )
```
